256 devices in a mesh: site: 4 (over y), sector: 64 (over x, z, core).
Axes of the slice: x: 4, y: 4, z: 8, core: 2. Of those that a mesh axis runs over, the one named last changes fastest.
Arguments:
- env_in: bfloat16 [2, 64, 512, 512], P(None, 'sector'), may hold values from -6 to 6
- bra: bfloat16 [4, 4, 64, 512, 512], P('site', None, 'sector'), may hold values from -0.25 to 0.25
- ket: bfloat16 [4, 2, 4, 64, 512, 512], P('site', None, None, 'sector'), may hold values from -0.125 to 0.125
- sector_dims: int32 [5, 64], replicated, may hold values from 384 to 512, as said below
- flags: int32 [4, 4, 64], P('site', None, 'sector'), may hold values 0 or 1
Outputs:
- env_after: bfloat16 [4, 2, 64, 512, 512], P('site', None, 'sector')
The draws below stay inside these ranges and needn't reach their ends.
Inputs may be any that keep to these rules, and one draw needn't show every extreme that they name: `sector_dims`: every bond has some sector whose used size is exactly 512.
All inputs are finite; a program needn't handle non-finite values. No bound on the sum of `flags` on one device may be relied on, other than what follows from the above.
Results may differ from the reference program's by a relative error of at most 0.013.
Values may be sent and summed in bfloat16 or wider, within the bound.
A program may use at most 64 MiB of HBM per device.

```python
import jax
import jax.numpy as jnp

P_SIZE = 512
PAIRS = 2
SECTORS = 64
N_SITE = 4


def draw_sector_dims(key, part):
    first_key = jax.random.fold_in(key, 11)
    second_key = jax.random.fold_in(key, 23)
    lowest = 3 * P_SIZE // 4
    dims = jax.random.randint(first_key, (N_SITE + 1, SECTORS), lowest, P_SIZE + 1)
    placed = jax.random.randint(second_key, (N_SITE + 1,), 0, SECTORS)
    column = jnp.arange(SECTORS)[None, :]
    dims = jnp.where(column == placed[:, None], P_SIZE, dims)
    return dims.astype(jnp.int32)


def touch_ends(array, key, low, largest):
    place = [jax.random.randint(jax.random.fold_in(key, axis), (), 0, length) for axis, length in enumerate(array.shape)]
    widest = array.shape.index(max(array.shape))
    beside = place[:widest] + [(place[widest] + 1) % array.shape[widest]] + place[widest + 1:]
    return array.at[tuple(place)].set(low).at[tuple(beside)].set(largest)


def shard_levels(rng, shape, pieces, low, high):
    loudness = 1.0
    for dim, shards_of in pieces:
        steps = jax.random.uniform(jax.random.fold_in(jax.random.fold_in(rng, 6), dim), (shards_of,), jnp.float32, low / len(pieces), high / len(pieces))
        loudness = loudness * jnp.repeat(jnp.exp(steps), shape[dim] // shards_of).reshape((-1,) + (1,) * (len(shape) - 1 - dim))
    return loudness


def normal_values(rng, shape, deviation, most, pieces=(), dtype=jnp.bfloat16):
    result = jax.random.normal(rng, shape, jnp.float32) * deviation
    if len(pieces) > 0:
        result = shard_levels(rng, shape, pieces, -0.22, 0.18) * result
    return jnp.clip(result, min=-most, max=most).astype(dtype)


def setup_inputs(seed: int = 0) -> dict:
    streams_of = jax.random.split(jax.random.key(seed), 6)
    return {
        "env_in": normal_values(streams_of[0], (PAIRS, SECTORS, P_SIZE, P_SIZE), 1.0, 6.0, ((1, 64),)),
        "bra": normal_values(streams_of[1], (N_SITE, 4, SECTORS, P_SIZE, P_SIZE), P_SIZE ** -0.5, 0.25, ((0, 4), (2, 64))),
        "ket": normal_values(streams_of[2], (N_SITE, PAIRS, 4, SECTORS, P_SIZE, P_SIZE), (4 * P_SIZE) ** -0.5, 0.125, ((0, 4), (3, 64))),
        "sector_dims": draw_sector_dims(jax.random.fold_in(streams_of[5], 71), 0),
        "flags": touch_ends((jax.random.randint(streams_of[4], (N_SITE, 4, SECTORS), 0, 4) < 3).astype(jnp.int32), jax.random.fold_in(streams_of[4], 1), 0, 1),
    }


def window_mask(sector_dims, bond):
    lanes = jnp.arange(P_SIZE)
    keep = (lanes[None, :] < sector_dims[bond][:, None]).astype(jnp.float32)
    return keep[:, :, None] * keep[:, None, :]


def raise_charge(blocks, amount):
    zeros = jnp.zeros((amount, P_SIZE, P_SIZE), jnp.float32)
    return jnp.concatenate([zeros, blocks[:-amount]], axis=0)


def reference(env_in, bra, ket, sector_dims, flags):
    first = window_mask(sector_dims, 0)
    envs = [(env_in[p].astype(jnp.float32) * first).astype(jnp.bfloat16) for p in range(PAIRS)]
    results = []
    for site_now in range(N_SITE):
        window = window_mask(sector_dims, site_now + 1)
        weights = flags[site_now].astype(jnp.float32)[:, :, None, None]
        layer = []
        for pair in range(PAIRS):
            moved = jnp.einsum("qab,sqbc->sqac", envs[pair].astype(jnp.float32), ket[site_now, pair].astype(jnp.float32)).astype(jnp.bfloat16)
            partial_value = jnp.einsum("sqba,sqbc->sqac", bra[site_now].astype(jnp.float32), moved.astype(jnp.float32)) * weights
            total = partial_value[0] + raise_charge(partial_value[1] + partial_value[2], 1) + raise_charge(partial_value[3], 2)
            fresh = (total * window).astype(jnp.bfloat16)
            layer.append(fresh)
            envs[pair] = fresh
        results.append(jnp.stack(layer, axis=0))
    return jnp.stack(results, axis=0)
```

```python
import jax
import jax.numpy as jnp
from jax import lax
from jax.experimental import pallas as pl
from jax.experimental.pallas import tpu as pltpu
from jax.sharding import PartitionSpec as P

MESH = pl.DeviceIdType.MESH
WIDE = 128
ROWS = 64
F32 = jnp.float32
BF16 = jnp.bfloat16


def chain_kernel(
    dims, flags, env, bra, ket, out,
    env_v, bra_v, ket_v, stay, three, s_out, s_in, x_out, x_in, e_out,
    env_sem, bra_sem, ket_sem, s_send, s_recv, x_send, x_recv, y_send, y_recv, o_sem,
):
    site, sector = lax.axis_index("site"), lax.axis_index("sector")
    sites, sectors = lax.axis_size("site"), lax.axis_size("sector")
    core = lax.rem(sector, 2)
    pairs, size = env_v.shape[0], env_v.shape[1]
    wides, chunks = size // WIDE, size // ROWS
    other = sector + 1 - 2 * core
    ahead = lax.rem(sector + 2, sectors)
    behind = lax.rem(sector + sectors - 2, sectors)
    first, last = site == 0, site == sites - 1

    def env_load(p):
        return pltpu.make_async_copy(env.at[p, 0], env_v.at[p], env_sem.at[p])

    def bra_load():
        return pltpu.make_async_copy(bra.at[0, :, 0], bra_v, bra_sem)

    def ket_load(p):
        return pltpu.make_async_copy(ket.at[0, p, :, 0], ket_v.at[p], ket_sem.at[p])

    def send_s(p, i):
        rows = pl.ds(pl.multiple_of(i * WIDE, WIDE), WIDE)
        return pltpu.make_async_remote_copy(
            s_out.at[p, rows], s_in.at[p, rows], s_send.at[p, i], s_recv.at[p, i],
            device_id=(site, other), device_id_type=MESH)

    def send_x(p, r):
        rows = pl.ds(pl.multiple_of(r * ROWS, ROWS), ROWS)
        return pltpu.make_async_remote_copy(
            x_out.at[p, rows], x_in.at[p, rows], x_send.at[p, r], x_recv.at[p, r],
            device_id=(site, ahead), device_id_type=MESH)

    def send_y(p, r):
        rows = pl.ds(pl.multiple_of(r * ROWS, ROWS), ROWS)
        return pltpu.make_async_remote_copy(
            e_out.at[p, rows], env_v.at[p, rows], y_send.at[p, r], y_recv.at[p, r],
            device_id=(lax.rem(site + 1, sites), sector), device_id_type=MESH)

    def store(p, r):
        rows = pl.ds(pl.multiple_of(r * ROWS, ROWS), ROWS)
        return pltpu.make_async_copy(e_out.at[p, rows], out.at[0, p, 0, rows], o_sem.at[p, r])

    barrier = pltpu.get_barrier_semaphore()
    for partner in (other, ahead, behind):
        pl.semaphore_signal(barrier, inc=1, device_id=(site, partner), device_id_type=MESH)
    for partner in (lax.rem(site + 1, sites), lax.rem(site + sites - 1, sites)):
        pl.semaphore_signal(barrier, inc=1, device_id=(partner, sector), device_id_type=MESH)

    @pl.when(first)
    def _():
        env_load(0).start()

    bra_load().start()
    ket_load(0).start()

    @pl.when(first)
    def _():
        env_load(1).start()

    ket_load(1).start()

    pl.semaphore_wait(barrier, 5)
    bra_load().wait()
    dim_first, dim_next = dims[0, sector], dims[site + 1, sector]
    on = [flags[0, s, 0].astype(F32) for s in range(4)]
    has_before = (sector >= 2).astype(jnp.int32)
    lane = lax.broadcasted_iota(jnp.int32, (ROWS, size), 1)
    row = lax.broadcasted_iota(jnp.int32, (ROWS, size), 0)

    def dot(a, b):
        return jnp.dot(a, b, preferred_element_type=F32)

    def x_of(p, i):
        send_s(p, i).wait_recv()
        rows = pl.ds(pl.multiple_of(i * WIDE, WIDE), WIDE)
        x_out[p, rows] = (three[rows] + s_in[p, rows].astype(F32)).astype(BF16)
        for k in range(WIDE // ROWS):
            send_x(p, i * (WIDE // ROWS) + k).start()

    def compute(p):
        ket_load(p).wait()

        @pl.when(first)
        def _():
            env_load(p).wait()

            def mask(r, carry):
                rows = pl.ds(pl.multiple_of(r * ROWS, ROWS), ROWS)
                inside = jnp.logical_and(row + r * ROWS < dim_first, lane < dim_first)
                env_v[p, rows] = jnp.where(inside, env_v[p, rows].astype(F32), 0.0).astype(BF16)
                return carry

            lax.fori_loop(0, chunks, mask, 0)

        @pl.when(jnp.logical_not(first))
        def _():
            def arrive(r, carry):
                send_y(p, r).wait_recv()
                return carry

            lax.fori_loop(0, chunks, arrive, 0)

        def step(i, carry):
            rows = pl.ds(pl.multiple_of(i * WIDE, WIDE), WIDE)
            here = env_v[p]
            left = [
                (lax.dot_general(bra_v[s, :, rows], here, (((0,), (0,)), ((), ())),
                                 preferred_element_type=F32) * on[s]).astype(BF16)
                for s in range(4)
            ]
            s_out[p, rows] = (dot(left[1], ket_v[p, 1]) + dot(left[2], ket_v[p, 2])).astype(BF16)
            send_s(p, i).start()
            double = dot(left[3], ket_v[p, 3])

            @pl.when(core == 1)
            def _():
                x_out[p, rows] = double.astype(BF16)
                for k in range(WIDE // ROWS):
                    send_x(p, i * (WIDE // ROWS) + k).start()

            @pl.when(core == 0)
            def _():
                three[rows] = double

            stay[p, rows] = dot(left[0], ket_v[p, 0])

            @pl.when(jnp.logical_and(core == 0, i > 0))
            def _():
                x_of(p, i - 1)

            return carry

        lax.fori_loop(0, wides, step, 0)

        @pl.when(core == 0)
        def _():
            x_of(p, wides - 1)

        @pl.when(core == 1)
        def _():
            def arrive(i, carry):
                send_s(p, i).wait_recv()
                rows = pl.ds(pl.multiple_of(i * WIDE, WIDE), WIDE)
                stay[p, rows] += s_in[p, rows].astype(F32)
                return carry

            lax.fori_loop(0, wides, arrive, 0)

    def finish(p):
        def step(r, carry):
            rows = pl.ds(pl.multiple_of(r * ROWS, ROWS), ROWS)
            send_x(p, r).wait_recv()
            arrived = jnp.where(has_before > 0, x_in[p, rows].astype(F32), 0.0)
            inside = jnp.logical_and(row + r * ROWS < dim_next, lane < dim_next)
            e_out[p, rows] = jnp.where(inside, stay[p, rows] + arrived, 0.0).astype(BF16)

            @pl.when(jnp.logical_not(last))
            def _():
                send_y(p, r).start()

            store(p, r).start()
            return carry

        lax.fori_loop(0, chunks, step, 0)

    def stage(t, carry):
        finishing = jnp.where(first, t // 2, lax.rem(t, 2))
        p = jnp.where(first, lax.rem(t, 2), t // 2)

        @pl.when(finishing == 0)
        def _():
            compute(p)

        @pl.when(finishing == 1)
        def _():
            finish(p)

        return carry

    lax.fori_loop(0, 2 * pairs, stage, 0)

    def drain(t, carry):
        p, r = t // chunks, lax.rem(t, chunks)
        send_x(p, r).wait_send()
        store(p, r).wait()

        @pl.when(jnp.logical_not(last))
        def _():
            send_y(p, r).wait_send()

        return carry

    lax.fori_loop(0, pairs * chunks, drain, 0)

    def drain_s(t, carry):
        send_s(t // wides, lax.rem(t, wides)).wait_send()
        return carry

    lax.fori_loop(0, pairs * wides, drain_s, 0)


def per_device(env_in, bra, ket, sector_dims, flags):
    pairs, size = env_in.shape[0], env_in.shape[-1]
    wides, chunks = size // WIDE, size // ROWS
    blocks = (pairs, size, size)
    dma = pltpu.SemaphoreType.DMA
    smem = pl.BlockSpec(memory_space=pltpu.SMEM)
    hbm = pl.BlockSpec(memory_space=pl.ANY)
    return pl.pallas_call(
        chain_kernel,
        out_shape=jax.ShapeDtypeStruct((1, pairs, 1, size, size), BF16),
        in_specs=[smem, smem, hbm, hbm, hbm],
        out_specs=hbm,
        scratch_shapes=[
            pltpu.VMEM(blocks, BF16),
            pltpu.VMEM((4, size, size), BF16),
            pltpu.VMEM((pairs, 4, size, size), BF16),
            pltpu.VMEM(blocks, F32),
            pltpu.VMEM((size, size), F32),
            pltpu.VMEM(blocks, BF16),
            pltpu.VMEM(blocks, BF16),
            pltpu.VMEM(blocks, BF16),
            pltpu.VMEM(blocks, BF16),
            pltpu.VMEM(blocks, BF16),
            dma((pairs,)),
            dma,
            dma((pairs,)),
            dma((pairs, wides)),
            dma((pairs, wides)),
            dma((pairs, chunks)),
            dma((pairs, chunks)),
            dma((pairs, chunks)),
            dma((pairs, chunks)),
            dma((pairs, chunks)),
        ],
        compiler_params=pltpu.CompilerParams(
            collective_id=0, has_side_effects=True, vmem_limit_bytes=56 << 20
        ),
        cost_estimate=pl.CostEstimate(
            flops=pairs * 16 * size**3, bytes_accessed=16 * size * size * 2, transcendentals=0
        ),
    )(sector_dims, flags, env_in, bra, ket)


def solution(mesh):
    in_specs = (
        P(None, "sector", None, None),
        P("site", None, "sector", None, None),
        P("site", None, None, "sector", None, None),
        P(),
        P("site", None, "sector"),
    )
    out_specs = P("site", None, "sector", None, None)
    return jax.shard_map(
        per_device, mesh=mesh, in_specs=in_specs, out_specs=out_specs, check_vma=False
    )
```

```python
import jax
import jax.numpy as jnp
from jax import lax
from jax.experimental import pallas as pl
from jax.experimental.pallas import tpu as pltpu
from jax.sharding import PartitionSpec as P

MESH = pl.DeviceIdType.MESH
WIDE = 128
ROWS = 64
TURN = 8
TURN_FIRST = 5
F32 = jnp.float32
BF16 = jnp.bfloat16


def chain_kernel(
    dims, flags, env, bra, ket, out,
    env_v, bra_v, ket_v, stay, three, s_out, s_in, x_out, x_in,
    env_sem, bra_sem, ket_sem, s_send, s_recv, x_send, x_recv, y_send, y_recv,
):
    site, sector = lax.axis_index("site"), lax.axis_index("sector")
    sites, sectors = lax.axis_size("site"), lax.axis_size("sector")
    core = lax.rem(sector, 2)
    pairs, size = env_v.shape[0], env_v.shape[1]
    wides, chunks = size // WIDE, size // ROWS
    other = sector + 1 - 2 * core
    ahead = lax.rem(sector + 2, sectors)
    behind = lax.rem(sector + sectors - 2, sectors)
    first, last = site == 0, site == sites - 1

    def env_load(p):
        return pltpu.make_async_copy(env.at[p, 0], env_v.at[p], env_sem.at[p])

    def bra_load(s):
        return pltpu.make_async_copy(bra.at[0, s, 0], bra_v.at[s], bra_sem.at[s])

    def ket_load(p, s):
        return pltpu.make_async_copy(ket.at[0, p, s, 0], ket_v.at[p, s], ket_sem.at[p, s])

    def send_s(p, i):
        rows = pl.ds(pl.multiple_of(i * WIDE, WIDE), WIDE)
        return pltpu.make_async_remote_copy(
            s_out.at[p, rows], s_in.at[p, rows], s_send.at[p, i], s_recv.at[p, i],
            device_id=(site, other), device_id_type=MESH)

    def send_x(p, r):
        rows = pl.ds(pl.multiple_of(r * ROWS, ROWS), ROWS)
        return pltpu.make_async_remote_copy(
            x_out.at[p, rows], x_in.at[p, rows], x_send.at[p, r], x_recv.at[p, r],
            device_id=(site, ahead), device_id_type=MESH)

    def send_y(p, r):
        rows = pl.ds(pl.multiple_of(r * ROWS, ROWS), ROWS)
        return pltpu.make_async_remote_copy(
            out.at[0, p, 0, rows], env_v.at[p, rows], y_send.at[p, r], y_recv.at[p, r],
            device_id=(lax.rem(site + 1, sites), sector), device_id_type=MESH)

    barrier = pltpu.get_barrier_semaphore()
    for partner in (other, ahead, behind):
        pl.semaphore_signal(barrier, inc=1, device_id=(site, partner), device_id_type=MESH)
    for partner in (lax.rem(site + 1, sites), lax.rem(site + sites - 1, sites)):
        pl.semaphore_signal(barrier, inc=1, device_id=(partner, sector), device_id_type=MESH)

    @pl.when(first)
    def _():
        env_load(0).start()

    for s in (3, 1, 2, 0):
        bra_load(s).start()
        ket_load(0, s).start()

    dim_first, dim_next = dims[0, sector], dims[site + 1, sector]
    on = [flags[0, 0, s].astype(F32) for s in range(4)]
    has_before = (sector >= 2).astype(jnp.int32)
    lane = lax.broadcasted_iota(jnp.int32, (ROWS, size), 1)
    row = lax.broadcasted_iota(jnp.int32, (ROWS, size), 0)

    def dot(a, b):
        return jnp.dot(a, b, preferred_element_type=F32)

    def x_of(p, i):
        send_s(p, i).wait_recv()
        rows = pl.ds(pl.multiple_of(i * WIDE, WIDE), WIDE)
        x_out[p, rows] = (three[rows] + s_in[p, rows].astype(F32)).astype(BF16)
        for k in range(WIDE // ROWS):
            send_x(p, i * (WIDE // ROWS) + k).start()

    def cover(p):
        @pl.when(first)
        def _():
            env_load(p).wait()

            def mask(r, carry):
                rows = pl.ds(pl.multiple_of(r * ROWS, ROWS), ROWS)
                inside = jnp.logical_and(row + r * ROWS < dim_first, lane < dim_first)
                env_v[p, rows] = jnp.where(inside, env_v[p, rows].astype(F32), 0.0).astype(BF16)
                return carry

            lax.fori_loop(0, chunks, mask, 0)

    def enter(p):
        @pl.when(jnp.logical_not(first))
        def _():
            def arrive(r, carry):
                send_y(p, r).wait_recv()
                return carry

            lax.fori_loop(0, chunks, arrive, 0)

    def compute(p, i):
        rows = pl.ds(pl.multiple_of(i * WIDE, WIDE), WIDE)
        here = env_v[p]

        def part(s):
            @pl.when(i == 0)
            def _():
                if p == 0:
                    bra_load(s).wait()
                ket_load(p, s).wait()

            left = lax.dot_general(bra_v[s, :, rows], here, (((0,), (0,)), ((), ())),
                                   preferred_element_type=F32)
            return dot((left * on[s]).astype(BF16), ket_v[p, s])

        def single():
            s_out[p, rows] = (part(1) + part(2)).astype(BF16)
            send_s(p, i).start()

        @pl.when(core == 1)
        def _():
            x_out[p, rows] = part(3).astype(BF16)
            for k in range(WIDE // ROWS):
                send_x(p, i * (WIDE // ROWS) + k).start()
            single()
            stay[p, rows] = part(0)

        @pl.when(core == 0)
        def _():
            single()
            three[rows] = part(3)

            @pl.when(jnp.logical_not(first))
            def _():
                x_of(p, i)

            stay[p, rows] = part(0)

            @pl.when(first)
            def _():
                @pl.when(i > 0)
                def _():
                    x_of(p, i - 1)

                @pl.when(i == wides - 1)
                def _():
                    x_of(p, i)

    def finish(p, r):
        rows = pl.ds(pl.multiple_of(r * ROWS, ROWS), ROWS)

        @pl.when(core == 1)
        def _():
            @pl.when(lax.rem(r, WIDE // ROWS) == 0)
            def _():
                send_s(p, r // (WIDE // ROWS)).wait_recv()

            stay[p, rows] += s_in[p, rows].astype(F32)

        send_x(p, r).wait_recv()
        arrived = jnp.where(has_before > 0, x_in[p, rows].astype(F32), 0.0)
        inside = jnp.logical_and(row + r * ROWS < dim_next, lane < dim_next)
        out[0, p, 0, rows] = jnp.where(inside, stay[p, rows] + arrived, 0.0).astype(BF16)

        @pl.when(jnp.logical_not(last))
        def _():
            send_y(p, r).start()

    turn = jnp.where(first, TURN_FIRST, TURN)

    def work(t, carry):
        k = t - turn

        @pl.when(jnp.logical_and(k >= 0, k < wides))
        def _():
            @pl.when(k == 0)
            def _():
                cover(1)
                enter(1)

            compute(1, k)

        @pl.when(t < chunks)
        def _():
            finish(0, t)

        return carry

    def first_compute(i, carry):
        compute(0, i)
        return carry

    def last_finish(r, carry):
        finish(1, r)
        return carry

    cover(0)
    pl.semaphore_wait(barrier, 5)
    enter(0)
    lax.fori_loop(0, wides, first_compute, 0)

    @pl.when(first)
    def _():
        env_load(1).start()

    for s in (3, 1, 2, 0):
        ket_load(1, s).start()
    lax.fori_loop(0, jnp.maximum(turn + wides, chunks), work, 0)
    lax.fori_loop(0, chunks, last_finish, 0)

    def drain(t, carry):
        p, r = t // chunks, lax.rem(t, chunks)
        send_x(p, r).wait_send()

        @pl.when(jnp.logical_not(last))
        def _():
            send_y(p, r).wait_send()

        return carry

    lax.fori_loop(0, pairs * chunks, drain, 0)

    def drain_s(t, carry):
        send_s(t // wides, lax.rem(t, wides)).wait_send()
        return carry

    lax.fori_loop(0, pairs * wides, drain_s, 0)


def per_device(env_in, bra, ket, sector_dims, flags):
    pairs, size = env_in.shape[0], env_in.shape[-1]
    wides, chunks = size // WIDE, size // ROWS
    blocks = (pairs, size, size)
    dma = pltpu.SemaphoreType.DMA
    smem = pl.BlockSpec(memory_space=pltpu.SMEM)
    hbm = pl.BlockSpec(memory_space=pl.ANY)
    return pl.pallas_call(
        chain_kernel,
        out_shape=pltpu.VMEM((1, pairs, 1, size, size), BF16),
        in_specs=[smem, smem, hbm, hbm, hbm],
        out_specs=pl.BlockSpec(memory_space=pltpu.VMEM),
        scratch_shapes=[
            pltpu.VMEM(blocks, BF16),
            pltpu.VMEM((4, size, size), BF16),
            pltpu.VMEM((pairs, 4, size, size), BF16),
            pltpu.VMEM(blocks, F32),
            pltpu.VMEM((size, size), F32),
            pltpu.VMEM(blocks, BF16),
            pltpu.VMEM(blocks, BF16),
            pltpu.VMEM(blocks, BF16),
            pltpu.VMEM(blocks, BF16),
            dma((pairs,)),
            dma((4,)),
            dma((pairs, 4)),
            dma((pairs, wides)),
            dma((pairs, wides)),
            dma((pairs, chunks)),
            dma((pairs, chunks)),
            dma((pairs, chunks)),
            dma((pairs, chunks)),
        ],
        compiler_params=pltpu.CompilerParams(
            collective_id=0, has_side_effects=True, vmem_limit_bytes=56 << 20
        ),
        cost_estimate=pl.CostEstimate(
            flops=pairs * 16 * size**3, bytes_accessed=16 * size * size * 2, transcendentals=0
        ),
    )(sector_dims, jnp.swapaxes(flags, 1, 2), env_in, bra, ket)


def solution(mesh):
    in_specs = (
        P(None, "sector", None, None),
        P("site", None, "sector", None, None),
        P("site", None, None, "sector", None, None),
        P(),
        P("site", None, "sector"),
    )
    out_specs = P("site", None, "sector", None, None)
    return jax.shard_map(
        per_device, mesh=mesh, in_specs=in_specs, out_specs=out_specs, check_vma=False
    )
```

```python
import jax
import jax.numpy as jnp
from jax import lax
from jax.experimental import pallas as pl
from jax.experimental.pallas import tpu as pltpu
from jax.sharding import PartitionSpec as P

MESH = pl.DeviceIdType.MESH
WIDE = 128
ROWS = 64
TURN = 8
TURN_ZERO = 8
TURN_ONE = 8
LATE = 5
F32 = jnp.float32
BF16 = jnp.bfloat16


def chain_kernel(
    dims, flags, env, bra, ket, out,
    env_v, bra_v, ket_v, moved, stay, three, s_out, s_in, x_out, x_in,
    env_sem, bra_sem, ket_sem, s_send, s_recv, x_send, x_recv, y_send, y_recv,
):
    site, sector = lax.axis_index("site"), lax.axis_index("sector")
    sites, sectors = lax.axis_size("site"), lax.axis_size("sector")
    core = lax.rem(sector, 2)
    pairs, size = env_v.shape[0], env_v.shape[1]
    wides, chunks = size // WIDE, size // ROWS
    other = sector + 1 - 2 * core
    ahead = lax.rem(sector + 2, sectors)
    behind = lax.rem(sector + sectors - 2, sectors)
    first, last = site == 0, site == sites - 1

    def env_load(p):
        return pltpu.make_async_copy(env.at[p, 0], env_v.at[p], env_sem.at[p])

    def bra_load(s):
        return pltpu.make_async_copy(bra.at[0, s, 0], bra_v.at[s], bra_sem.at[s])

    def ket_load(p, s):
        return pltpu.make_async_copy(ket.at[0, p, s, 0], ket_v.at[p, s], ket_sem.at[p, s])

    def send_s(p, i):
        rows = pl.ds(pl.multiple_of(i * WIDE, WIDE), WIDE)
        return pltpu.make_async_remote_copy(
            s_out.at[p, rows], s_in.at[p, rows], s_send.at[p, i], s_recv.at[p, i],
            device_id=(site, other), device_id_type=MESH)

    def send_x(p, r):
        rows = pl.ds(pl.multiple_of(r * ROWS, ROWS), ROWS)
        return pltpu.make_async_remote_copy(
            x_out.at[p, rows], x_in.at[p, rows], x_send.at[p, r], x_recv.at[p, r],
            device_id=(site, ahead), device_id_type=MESH)

    def send_y(p, r):
        rows = pl.ds(pl.multiple_of(r * ROWS, ROWS), ROWS)
        return pltpu.make_async_remote_copy(
            out.at[0, p, 0, rows], env_v.at[p, rows], y_send.at[p, r], y_recv.at[p, r],
            device_id=(lax.rem(site + 1, sites), sector), device_id_type=MESH)

    barrier = pltpu.get_barrier_semaphore()
    for partner in (other, ahead, behind):
        pl.semaphore_signal(barrier, inc=1, device_id=(site, partner), device_id_type=MESH)
    for partner in (lax.rem(site + 1, sites), lax.rem(site + sites - 1, sites)):
        pl.semaphore_signal(barrier, inc=1, device_id=(partner, sector), device_id_type=MESH)

    @pl.when(first)
    def _():
        env_load(0).start()

    for s in (3, 1, 2, 0):
        bra_load(s).start()
        ket_load(0, s).start()

    dim_first, dim_next = dims[0, sector], dims[site + 1, sector]
    on = [flags[0, 0, s].astype(F32) for s in range(4)]
    has_before = (sector >= 2).astype(jnp.int32)
    lane = lax.broadcasted_iota(jnp.int32, (ROWS, size), 1)
    row = lax.broadcasted_iota(jnp.int32, (ROWS, size), 0)

    def dot(a, b):
        return jnp.dot(a, b, preferred_element_type=F32)

    def x_of(p, i):
        send_s(p, i).wait_recv()
        rows = pl.ds(pl.multiple_of(i * WIDE, WIDE), WIDE)
        x_out[p, rows] = (three[rows] + s_in[p, rows].astype(F32)).astype(BF16)
        for k in range(WIDE // ROWS):
            send_x(p, i * (WIDE // ROWS) + k).start()

    def cover(p):
        @pl.when(first)
        def _():
            env_load(p).wait()

            def mask(r, carry):
                rows = pl.ds(pl.multiple_of(r * ROWS, ROWS), ROWS)
                inside = jnp.logical_and(row + r * ROWS < dim_first, lane < dim_first)
                env_v[p, rows] = jnp.where(inside, env_v[p, rows].astype(F32), 0.0).astype(BF16)
                return carry

            lax.fori_loop(0, chunks, mask, 0)

    def arrive(p, i):
        for k in range(WIDE // ROWS):
            send_y(p, i * (WIDE // ROWS) + k).wait_recv()

    def move(p, s, i):
        rows = pl.ds(pl.multiple_of(i * WIDE, WIDE), WIDE)
        moved[s, rows] = (dot(env_v[p, rows], ket_v[p, s]) * on[s]).astype(BF16)

    def early(p, i):
        arrive(p, i)
        for s in range(4):
            move(p, s, i)

    def rest(p, s):
        move(p, s, wides - 1)

    def part(s, rows):
        return lax.dot_general(bra_v[s, :, rows], moved[s], (((0,), (0,)), ((), ())),
                               preferred_element_type=F32)

    def by_chunk(body):
        def step(i, carry):
            body(i, pl.ds(pl.multiple_of(i * WIDE, WIDE), WIDE))
            return carry

        lax.fori_loop(0, wides, step, 0)

    def single(p):
        def body(i, rows):
            s_out[p, rows] = (part(1, rows) + part(2, rows)).astype(BF16)
            send_s(p, i).start()

        by_chunk(body)

    def double(p):
        rest(p, 3)

        def body(i, rows):
            both = part(3, rows)

            @pl.when(core == 1)
            def _():
                x_out[p, rows] = both.astype(BF16)
                for k in range(WIDE // ROWS):
                    send_x(p, i * (WIDE // ROWS) + k).start()

            @pl.when(core == 0)
            def _():
                three[rows] = both
                x_of(p, i)

        by_chunk(body)

    def none(p):
        rest(p, 0)

        def body(i, rows):
            stay[p, rows] = part(0, rows)

        by_chunk(body)

    def compute_first(p, i):
        rows = pl.ds(pl.multiple_of(i * WIDE, WIDE), WIDE)
        here = env_v[p]

        def whole(s):
            @pl.when(i == 0)
            def _():
                if p == 0:
                    bra_load(s).wait()
                ket_load(p, s).wait()

            left = lax.dot_general(bra_v[s, :, rows], here, (((0,), (0,)), ((), ())),
                                   preferred_element_type=F32)
            return dot((left * on[s]).astype(BF16), ket_v[p, s])

        both = whole(3)

        @pl.when(core == 1)
        def _():
            x_out[p, rows] = both.astype(BF16)
            for k in range(WIDE // ROWS):
                send_x(p, i * (WIDE // ROWS) + k).start()

        @pl.when(core == 0)
        def _():
            three[rows] = both

        s_out[p, rows] = (whole(1) + whole(2)).astype(BF16)
        send_s(p, i).start()
        stay[p, rows] = whole(0)

        @pl.when(jnp.logical_and(core == 0, i > 0))
        def _():
            x_of(p, i - 1)

        @pl.when(jnp.logical_and(core == 0, i == wides - 1))
        def _():
            x_of(p, i)

    def compute_later(p, k):
        @pl.when(k == 0)
        def _():
            arrive(p, wides - 1)

        @pl.when(jnp.where(core == 1, k == 0, k == 2))
        def _():
            double(p)

        @pl.when(jnp.where(core == 1, k == 1, k == 0))
        def _():
            rest(p, 1)
            rest(p, 2)

        @pl.when(jnp.where(core == 1, k == 2, k == 1))
        def _():
            single(p)

        @pl.when(k == 3)
        def _():
            none(p)

    def compute(p, k):
        @pl.when(first)
        def _():
            compute_first(p, k)

        @pl.when(jnp.logical_not(first))
        def _():
            compute_later(p, k)

    def finish(p, r):
        rows = pl.ds(pl.multiple_of(r * ROWS, ROWS), ROWS)

        @pl.when(jnp.logical_and(core == 1, lax.rem(r, WIDE // ROWS) == 0))
        def _():
            send_s(p, r // (WIDE // ROWS)).wait_recv()

        send_x(p, r).wait_recv()
        total = stay[p, rows] + jnp.where(core == 1, s_in[p, rows].astype(F32), 0.0)
        total += jnp.where(has_before > 0, x_in[p, rows].astype(F32), 0.0)
        inside = jnp.logical_and(row + r * ROWS < dim_next, lane < dim_next)
        out[0, p, 0, rows] = jnp.where(inside, total, 0.0).astype(BF16)

        @pl.when(jnp.logical_not(last))
        def _():
            send_y(p, r).start()

    turn = jnp.where(first, jnp.where(core == 1, TURN_ONE, TURN_ZERO), TURN)

    def work(t, carry):
        k = t - turn

        @pl.when(jnp.logical_and(k >= 0, k < 4))
        def _():
            @pl.when(k == 0)
            def _():
                cover(1)

            compute(1, k)

        @pl.when(t < chunks)
        def _():
            finish(0, t)

        i = t - LATE

        @pl.when(jnp.logical_and(jnp.logical_not(first), jnp.logical_and(i >= 0, i < wides - 1)))
        def _():
            @pl.when(i == 0)
            def _():
                for s in range(4):
                    ket_load(1, s).wait()

            early(1, i)

        return carry

    def first_early(i, carry):
        early(0, i)
        return carry

    def first_compute(k, carry):
        compute(0, k)
        return carry

    def last_finish(r, carry):
        finish(1, r)
        return carry

    cover(0)
    pl.semaphore_wait(barrier, 5)

    @pl.when(jnp.logical_not(first))
    def _():
        for s in range(4):
            ket_load(0, s).wait()
            bra_load(s).wait()
        lax.fori_loop(0, wides - 1, first_early, 0)

    lax.fori_loop(0, 4, first_compute, 0)

    @pl.when(first)
    def _():
        env_load(1).start()

    for s in (3, 1, 2, 0):
        ket_load(1, s).start()

    lax.fori_loop(0, jnp.maximum(turn + 4, chunks), work, 0)
    lax.fori_loop(0, chunks, last_finish, 0)

    def drain(t, carry):
        p, r = t // chunks, lax.rem(t, chunks)
        send_x(p, r).wait_send()

        @pl.when(jnp.logical_not(last))
        def _():
            send_y(p, r).wait_send()

        return carry

    lax.fori_loop(0, pairs * chunks, drain, 0)

    def drain_s(t, carry):
        send_s(t // wides, lax.rem(t, wides)).wait_send()
        return carry

    lax.fori_loop(0, pairs * wides, drain_s, 0)


def per_device(env_in, bra, ket, sector_dims, flags):
    pairs, size = env_in.shape[0], env_in.shape[-1]
    wides, chunks = size // WIDE, size // ROWS
    blocks = (pairs, size, size)
    dma = pltpu.SemaphoreType.DMA
    smem = pl.BlockSpec(memory_space=pltpu.SMEM)
    hbm = pl.BlockSpec(memory_space=pl.ANY)
    return pl.pallas_call(
        chain_kernel,
        out_shape=pltpu.VMEM((1, pairs, 1, size, size), BF16),
        in_specs=[smem, smem, hbm, hbm, hbm],
        out_specs=pl.BlockSpec(memory_space=pltpu.VMEM),
        scratch_shapes=[
            pltpu.VMEM(blocks, BF16),
            pltpu.VMEM((4, size, size), BF16),
            pltpu.VMEM((pairs, 4, size, size), BF16),
            pltpu.VMEM((4, size, size), BF16),
            pltpu.VMEM(blocks, F32),
            pltpu.VMEM((size, size), F32),
            pltpu.VMEM(blocks, BF16),
            pltpu.VMEM(blocks, BF16),
            pltpu.VMEM(blocks, BF16),
            pltpu.VMEM(blocks, BF16),
            dma((pairs,)),
            dma((4,)),
            dma((pairs, 4)),
            dma((pairs, wides)),
            dma((pairs, wides)),
            dma((pairs, chunks)),
            dma((pairs, chunks)),
            dma((pairs, chunks)),
            dma((pairs, chunks)),
        ],
        compiler_params=pltpu.CompilerParams(
            collective_id=0, has_side_effects=True, vmem_limit_bytes=56 << 20
        ),
        cost_estimate=pl.CostEstimate(
            flops=pairs * 16 * size**3, bytes_accessed=16 * size * size * 2, transcendentals=0
        ),
    )(sector_dims, jnp.swapaxes(flags, 1, 2), env_in, bra, ket)


def solution(mesh):
    in_specs = (
        P(None, "sector", None, None),
        P("site", None, "sector", None, None),
        P("site", None, None, "sector", None, None),
        P(),
        P("site", None, "sector"),
    )
    out_specs = P("site", None, "sector", None, None)
    return jax.shard_map(
        per_device, mesh=mesh, in_specs=in_specs, out_specs=out_specs, check_vma=False
    )
```

```python
import jax
import jax.numpy as jnp
from jax import lax
from jax.experimental import pallas as pl
from jax.experimental.pallas import tpu as pltpu
from jax.sharding import PartitionSpec as P

MESH = pl.DeviceIdType.MESH
WIDE = 128
HALF = 256
ROWS = 64
TURN = 8
TURN_ZERO = 3
TURN_ONE = 4
RELAYED = 3
LATE = 5
F32 = jnp.float32
BF16 = jnp.bfloat16


def chain_kernel(
    dims, flags, env, bra, ket, out,
    env_v, bra_v, ket_v, moved, stay, three, s_out, s_in, x_out, x_in,
    env_sem, bra_sem, ket_sem, s_send, s_recv, x_send, x_recv, y_send, y_recv,
    relay, relay_send, relay_recv,
):
    site, sector = lax.axis_index("site"), lax.axis_index("sector")
    sites, sectors = lax.axis_size("site"), lax.axis_size("sector")
    core = lax.rem(sector, 2)
    pairs, size = env_v.shape[0], env_v.shape[1]
    wides, chunks = size // WIDE, size // ROWS
    other = sector + 1 - 2 * core
    ahead = lax.rem(sector + 2, sectors)
    behind = lax.rem(sector + sectors - 2, sectors)
    first, last = site == 0, site == sites - 1

    def env_load(p):
        return pltpu.make_async_copy(env.at[p, 0], env_v.at[p], env_sem.at[p])

    def bra_load(s):
        return pltpu.make_async_copy(bra.at[0, s, 0], bra_v.at[s], bra_sem.at[s])

    def ket_load(p, s):
        return pltpu.make_async_copy(ket.at[0, p, s, 0], ket_v.at[p, s], ket_sem.at[p, s])

    def send_s(p, i):
        rows = pl.ds(pl.multiple_of(i * WIDE, WIDE), WIDE)
        return pltpu.make_async_remote_copy(
            s_out.at[p, rows], s_in.at[p, rows], s_send.at[p, i], s_recv.at[p, i],
            device_id=(site, other), device_id_type=MESH)

    def send_x(p, r):
        rows = pl.ds(pl.multiple_of(r * ROWS, ROWS), ROWS)
        return pltpu.make_async_remote_copy(
            x_out.at[p, rows], x_in.at[p, rows], x_send.at[p, r], x_recv.at[p, r],
            device_id=(site, ahead), device_id_type=MESH)

    def detour(p, r):
        sends = (site == 1) if p == 0 else jnp.logical_or(site == 1, site == 2)
        return jnp.logical_and(jnp.logical_and(core == 1, r < RELAYED), sends)

    def send_y(p, r):
        rows = pl.ds(pl.multiple_of(r * ROWS, ROWS), ROWS)
        return pltpu.make_async_remote_copy(
            out.at[0, p, 0, rows], env_v.at[p, rows], y_send.at[p, r], y_recv.at[p, r],
            device_id=(lax.rem(site + 1, sites), sector), device_id_type=MESH)

    def send_relay(p, r):
        rows = pl.ds(pl.multiple_of(r * ROWS, ROWS), ROWS)
        return pltpu.make_async_remote_copy(
            out.at[0, p, 0, rows], relay.at[p, rows], y_send.at[p, r], relay_recv.at[p, r],
            device_id=(jnp.where(site == 1, 3, 1), jnp.where(site == 1, other, sector)), device_id_type=MESH)

    def send_on(p, r):
        rows = pl.ds(pl.multiple_of(r * ROWS, ROWS), ROWS)
        return pltpu.make_async_remote_copy(
            relay.at[p, rows], env_v.at[p, rows], relay_send.at[p, r], y_recv.at[p, r],
            device_id=(jnp.where(site == 3, 2, 3), jnp.where(site == 3, other, sector)), device_id_type=MESH)

    def pass_on(p):
        def body(r, carry):
            send_relay(p, r).wait_recv()
            send_on(p, r).start()
            return carry

        lax.fori_loop(0, RELAYED, body, 0)

    def passed_on(p):
        def body(r, carry):
            send_on(p, r).wait_send()
            return carry

        lax.fori_loop(0, RELAYED, body, 0)

    barrier = pltpu.get_barrier_semaphore()
    for partner in (other, ahead, behind):
        pl.semaphore_signal(barrier, inc=1, device_id=(site, partner), device_id_type=MESH)
    for partner in (lax.rem(site + 1, sites), lax.rem(site + sites - 1, sites)):
        pl.semaphore_signal(barrier, inc=1, device_id=(partner, sector), device_id_type=MESH)
    pl.semaphore_signal(barrier, inc=1, device_id=(lax.rem(site + 2, sites), other), device_id_type=MESH)

    @pl.when(first)
    def _():
        env_load(0).start()

    for s in (3, 1, 2, 0):
        bra_load(s).start()
        ket_load(0, s).start()

    dim_first, dim_next = dims[0, sector], dims[site + 1, sector]
    on = [flags[0, 0, s].astype(F32) for s in range(4)]
    has_before = (sector >= 2).astype(jnp.int32)
    lane = lax.broadcasted_iota(jnp.int32, (ROWS, size), 1)
    row = lax.broadcasted_iota(jnp.int32, (ROWS, size), 0)

    def dot(a, b):
        return jnp.dot(a, b, preferred_element_type=F32)

    def x_of(p, i):
        send_s(p, i).wait_recv()
        rows = pl.ds(pl.multiple_of(i * WIDE, WIDE), WIDE)
        x_out[p, rows] = (three[rows] + s_in[p, rows].astype(F32)).astype(BF16)
        for k in range(WIDE // ROWS):
            send_x(p, i * (WIDE // ROWS) + k).start()

    def cover(p):
        @pl.when(first)
        def _():
            env_load(p).wait()

            def mask(r, carry):
                rows = pl.ds(pl.multiple_of(r * ROWS, ROWS), ROWS)
                inside = jnp.logical_and(row + r * ROWS < dim_first, lane < dim_first)
                env_v[p, rows] = jnp.where(inside, env_v[p, rows].astype(F32), 0.0).astype(BF16)
                return carry

            lax.fori_loop(0, chunks, mask, 0)

    def arrive(p, i):
        for k in range(WIDE // ROWS):
            send_y(p, i * (WIDE // ROWS) + k).wait_recv()

    def move(p, s, i):
        rows = pl.ds(pl.multiple_of(i * WIDE, WIDE), WIDE)
        moved[s, rows] = (dot(env_v[p, rows], ket_v[p, s]) * on[s]).astype(BF16)

    def early(p, i):
        arrive(p, i)
        for s in range(4):
            move(p, s, i)

    def part(s, rows):
        return lax.dot_general(bra_v[s, :, rows], moved[s], (((0,), (0,)), ((), ())),
                               preferred_element_type=F32)

    def by_half(body):
        def step(h, carry):
            body(h, pl.ds(pl.multiple_of(h * HALF, HALF), HALF))
            return carry

        lax.fori_loop(0, size // HALF, step, 0)

    def single(p):
        def body(h, rows):
            s_out[p, rows] = (part(1, rows) + part(2, rows)).astype(BF16)
            for k in range(HALF // WIDE):
                send_s(p, h * (HALF // WIDE) + k).start()

        by_half(body)

    def double(p):
        def body(h, rows):
            both = part(3, rows)
            x_out[p, rows] = both.astype(BF16)
            three[rows] = both

            @pl.when(core == 1)
            def _():
                for k in range(HALF // ROWS):
                    send_x(p, h * (HALF // ROWS) + k).start()

            @pl.when(core == 0)
            def _():
                for k in range(HALF // WIDE):
                    x_of(p, h * (HALF // WIDE) + k)

        by_half(body)

    def none(p):
        def body(h, rows):
            stay[p, rows] = part(0, rows)

        by_half(body)

    def compute_first(p, i):
        rows = pl.ds(pl.multiple_of(i * WIDE, WIDE), WIDE)
        here = env_v[p]

        @pl.when(i == 0)
        def _():
            for s in (3, 1, 2, 0):
                if p == 0:
                    bra_load(s).wait()
                ket_load(p, s).wait()

        def whole(s):
            left = lax.dot_general(bra_v[s, :, rows], here, (((0,), (0,)), ((), ())),
                                   preferred_element_type=F32)
            return dot((left * on[s]).astype(BF16), ket_v[p, s])

        both = whole(3)
        x_out[p, rows] = both.astype(BF16)
        three[rows] = both
        s_out[p, rows] = (whole(1) + whole(2)).astype(BF16)
        stay[p, rows] = whole(0)
        send_s(p, i).start()
        if p == 0:
            @pl.when(core == 1)
            def _():
                for k in range(WIDE // ROWS):
                    send_x(p, i * (WIDE // ROWS) + k).start()

        @pl.when(jnp.logical_and(core == 0, i > 0))
        def _():
            x_of(p, i - 1)

        @pl.when(jnp.logical_and(core == 0, i == wides - 1))
        def _():
            x_of(p, i)

    def compute_later(p, k):
        @pl.when(k == 0)
        def _():
            arrive(p, wides - 1)
            for s in (1, 2, 3, 0):
                move(p, s, wides - 1)

        @pl.when(jnp.where(core == 1, k == 2, k == 1))
        def _():
            single(p)

        @pl.when(jnp.where(core == 1, k == 1, k == 2))
        def _():
            double(p)

        @pl.when(k == 3)
        def _():
            none(p)

    def compute(p, k):
        @pl.when(first)
        def _():
            compute_first(p, k)

        @pl.when(jnp.logical_not(first))
        def _():
            compute_later(p, k)

    def finish(p, r):
        rows = pl.ds(pl.multiple_of(r * ROWS, ROWS), ROWS)

        told = jnp.logical_and(core == 1, lax.rem(r, WIDE // ROWS) == 0)
        if p == 1:
            told = jnp.logical_and(told, jnp.logical_not(jnp.logical_and(first, r == 0)))

        @pl.when(told)
        def _():
            send_s(p, r // (WIDE // ROWS)).wait_recv()

        send_x(p, r).wait_recv()
        total = stay[p, rows] + jnp.where(core == 1, s_in[p, rows].astype(F32), 0.0)
        total += jnp.where(has_before > 0, x_in[p, rows].astype(F32), 0.0)
        inside = jnp.logical_and(row + r * ROWS < dim_next, lane < dim_next)
        out[0, p, 0, rows] = jnp.where(inside, total, 0.0).astype(BF16)

        around = detour(p, r)

        @pl.when(around)
        def _():
            send_relay(p, r).start()

        @pl.when(jnp.logical_not(jnp.logical_or(last, around)))
        def _():
            send_y(p, r).start()

    turn = jnp.where(first, jnp.where(core == 1, TURN_ONE, TURN_ZERO), TURN)

    def work(t, carry):
        k = t - turn

        @pl.when(jnp.logical_and(k >= 0, k < 4))
        def _():
            @pl.when(k == 0)
            def _():
                cover(1)

            compute(1, k)

        @pl.when(t < chunks)
        def _():
            finish(0, t)

        i = t - LATE

        @pl.when(jnp.logical_and(jnp.logical_not(first), jnp.logical_and(i >= 0, i < wides - 1)))
        def _():
            @pl.when(i == 0)
            def _():
                for s in range(4):
                    ket_load(1, s).wait()

            early(1, i)

        return carry

    def first_early(i, carry):
        early(0, i)
        return carry

    def first_compute(k, carry):
        compute(0, k)
        return carry

    def last_finish(r, carry):
        finish(1, r)
        return carry

    cover(0)
    pl.semaphore_wait(barrier, 6)

    @pl.when(jnp.logical_and(site == 3, core == 0))
    def _():
        pass_on(0)
        pass_on(1)

    @pl.when(jnp.logical_not(first))
    def _():
        for s in range(4):
            ket_load(0, s).wait()
            bra_load(s).wait()
        lax.fori_loop(0, wides - 1, first_early, 0)

    lax.fori_loop(0, 4, first_compute, 0)

    @pl.when(first)
    def _():
        env_load(1).start()

    for s in (3, 1, 2, 0):
        ket_load(1, s).start()

    lax.fori_loop(0, jnp.maximum(turn + 4, chunks), work, 0)

    @pl.when(jnp.logical_and(first, core == 1))
    def _():
        send_s(1, 0).wait_recv()

        def send(r, carry):
            send_x(1, r).start()
            return carry

        lax.fori_loop(0, chunks, send, 0)

    lax.fori_loop(0, chunks, last_finish, 0)

    @pl.when(jnp.logical_and(site == 1, core == 1))
    def _():
        pass_on(1)
        passed_on(1)

    @pl.when(jnp.logical_and(site == 3, core == 0))
    def _():
        passed_on(0)
        passed_on(1)

    def drain(t, carry):
        p, r = t // chunks, lax.rem(t, chunks)
        send_x(p, r).wait_send()

        @pl.when(jnp.logical_not(last))
        def _():
            send_y(p, r).wait_send()

        return carry

    lax.fori_loop(0, pairs * chunks, drain, 0)

    def drain_s(t, carry):
        send_s(t // wides, lax.rem(t, wides)).wait_send()
        return carry

    lax.fori_loop(0, pairs * wides, drain_s, 0)


def per_device(env_in, bra, ket, sector_dims, flags):
    pairs, size = env_in.shape[0], env_in.shape[-1]
    wides, chunks = size // WIDE, size // ROWS
    blocks = (pairs, size, size)
    dma = pltpu.SemaphoreType.DMA
    smem = pl.BlockSpec(memory_space=pltpu.SMEM)
    hbm = pl.BlockSpec(memory_space=pl.ANY)
    return pl.pallas_call(
        chain_kernel,
        out_shape=pltpu.VMEM((1, pairs, 1, size, size), BF16),
        in_specs=[smem, smem, hbm, hbm, hbm],
        out_specs=pl.BlockSpec(memory_space=pltpu.VMEM),
        scratch_shapes=[
            pltpu.VMEM(blocks, BF16),
            pltpu.VMEM((4, size, size), BF16),
            pltpu.VMEM((pairs, 4, size, size), BF16),
            pltpu.VMEM((4, size, size), BF16),
            pltpu.VMEM(blocks, F32),
            pltpu.VMEM((size, size), F32),
            pltpu.VMEM(blocks, BF16),
            pltpu.VMEM(blocks, BF16),
            pltpu.VMEM(blocks, BF16),
            pltpu.VMEM(blocks, BF16),
            dma((pairs,)),
            dma((4,)),
            dma((pairs, 4)),
            dma((pairs, wides)),
            dma((pairs, wides)),
            dma((pairs, chunks)),
            dma((pairs, chunks)),
            dma((pairs, chunks)),
            dma((pairs, chunks)),
            pltpu.VMEM((pairs, RELAYED * ROWS, size), BF16),
            dma((pairs, RELAYED)),
            dma((pairs, RELAYED)),
        ],
        compiler_params=pltpu.CompilerParams(
            collective_id=0, has_side_effects=True, vmem_limit_bytes=56 << 20
        ),
        cost_estimate=pl.CostEstimate(
            flops=pairs * 16 * size**3, bytes_accessed=16 * size * size * 2, transcendentals=0
        ),
    )(sector_dims, jnp.swapaxes(flags, 1, 2), env_in, bra, ket)


def solution(mesh):
    in_specs = (
        P(None, "sector", None, None),
        P("site", None, "sector", None, None),
        P("site", None, None, "sector", None, None),
        P(),
        P("site", None, "sector"),
    )
    out_specs = P("site", None, "sector", None, None)
    return jax.shard_map(
        per_device, mesh=mesh, in_specs=in_specs, out_specs=out_specs, check_vma=False
    )
```

```python
import jax
import jax.numpy as jnp
from jax import lax
from jax.experimental import pallas as pl
from jax.experimental.pallas import tpu as pltpu
from jax.sharding import PartitionSpec as P

MESH = pl.DeviceIdType.MESH
WIDE = 128
HALF = 256
ROWS = 64
TURN = 8
TURN_ZERO = 4
TURN_ONE = 4
X_FIRST = 6
X_LAST = 2
RELAYED = 3
LATE = 5
F32 = jnp.float32
BF16 = jnp.bfloat16


def chain_kernel(
    dims, flags, env, bra, ket, out,
    env_v, bra_v, ket_v, moved, stay, three, s_out, s_in, x_out, x_in,
    env_sem, bra_sem, ket_sem, s_send, s_recv, x_send, x_recv, y_send, y_recv,
    relay, relay_send, relay_recv, x_relay, xr_send, xr_recv,
):
    site, sector = lax.axis_index("site"), lax.axis_index("sector")
    sites, sectors = lax.axis_size("site"), lax.axis_size("sector")
    core = lax.rem(sector, 2)
    pairs, size = env_v.shape[0], env_v.shape[1]
    wides, chunks = size // WIDE, size // ROWS
    other = sector + 1 - 2 * core
    ahead = lax.rem(sector + 2, sectors)
    behind = lax.rem(sector + sectors - 2, sectors)
    first, last = site == 0, site == sites - 1

    def env_load(p):
        return pltpu.make_async_copy(env.at[p, 0], env_v.at[p], env_sem.at[p])

    def bra_load(s):
        return pltpu.make_async_copy(bra.at[0, s, 0], bra_v.at[s], bra_sem.at[s])

    def ket_load(p, s):
        return pltpu.make_async_copy(ket.at[0, p, s, 0], ket_v.at[p, s], ket_sem.at[p, s])

    def send_s(p, i):
        rows = pl.ds(pl.multiple_of(i * WIDE, WIDE), WIDE)
        return pltpu.make_async_remote_copy(
            s_out.at[p, rows], s_in.at[p, rows], s_send.at[p, i], s_recv.at[p, i],
            device_id=(site, other), device_id_type=MESH)

    def send_x(p, r):
        rows = pl.ds(pl.multiple_of(r * ROWS, ROWS), ROWS)
        return pltpu.make_async_remote_copy(
            x_out.at[p, rows], x_in.at[p, rows], x_send.at[p, r], x_recv.at[p, r],
            device_id=(site, ahead), device_id_type=MESH)

    def detour(p, r):
        sends = (site == 1) if p == 0 else jnp.logical_or(site == 1, site == 2)
        return jnp.logical_and(jnp.logical_and(core == 1, r < RELAYED), sends)

    def send_y(p, r):
        rows = pl.ds(pl.multiple_of(r * ROWS, ROWS), ROWS)
        return pltpu.make_async_remote_copy(
            out.at[0, p, 0, rows], env_v.at[p, rows], y_send.at[p, r], y_recv.at[p, r],
            device_id=(lax.rem(site + 1, sites), sector), device_id_type=MESH)

    def send_relay(p, r):
        rows = pl.ds(pl.multiple_of(r * ROWS, ROWS), ROWS)
        return pltpu.make_async_remote_copy(
            out.at[0, p, 0, rows], relay.at[p, rows], y_send.at[p, r], relay_recv.at[p, r],
            device_id=(jnp.where(site == 1, 3, 1), jnp.where(site == 1, other, sector)), device_id_type=MESH)

    def send_on(p, r):
        rows = pl.ds(pl.multiple_of(r * ROWS, ROWS), ROWS)
        return pltpu.make_async_remote_copy(
            relay.at[p, rows], env_v.at[p, rows], relay_send.at[p, r], y_recv.at[p, r],
            device_id=(jnp.where(site == 3, 2, 3), jnp.where(site == 3, other, sector)), device_id_type=MESH)

    def pass_on(p):
        def body(r, carry):
            send_relay(p, r).wait_recv()
            send_on(p, r).start()
            return carry

        lax.fori_loop(0, RELAYED, body, 0)

    def passed_on(p):
        def body(r, carry):
            send_on(p, r).wait_send()
            return carry

        lax.fori_loop(0, RELAYED, body, 0)

    barrier = pltpu.get_barrier_semaphore()
    for partner in (other, ahead, behind):
        pl.semaphore_signal(barrier, inc=1, device_id=(site, partner), device_id_type=MESH)
    for partner in (lax.rem(site + 1, sites), lax.rem(site + sites - 1, sites)):
        pl.semaphore_signal(barrier, inc=1, device_id=(partner, sector), device_id_type=MESH)
    pl.semaphore_signal(barrier, inc=1, device_id=(lax.rem(site + 2, sites), other), device_id_type=MESH)

    @pl.when(first)
    def _():
        env_load(0).start()

    for s in (3, 1, 2, 0):
        bra_load(s).start()
        ket_load(0, s).start()

    dim_first, dim_next = dims[0, sector], dims[site + 1, sector]
    on = [flags[0, 0, s].astype(F32) for s in range(4)]
    has_before = (sector >= 2).astype(jnp.int32)
    lane = lax.broadcasted_iota(jnp.int32, (ROWS, size), 1)
    row = lax.broadcasted_iota(jnp.int32, (ROWS, size), 0)

    def dot(a, b):
        return jnp.dot(a, b, preferred_element_type=F32)

    def send_xr(r):
        rows = pl.ds(pl.multiple_of(r * ROWS, ROWS), ROWS)
        return pltpu.make_async_remote_copy(
            x_out.at[1, rows], x_relay.at[rows], x_send.at[1, r], xr_recv.at[r],
            device_id=(jnp.where(site == 0, 3, 0), sector), device_id_type=MESH)

    def send_xon(r):
        rows = pl.ds(pl.multiple_of(r * ROWS, ROWS), ROWS)
        return pltpu.make_async_remote_copy(
            x_relay.at[rows], x_in.at[1, rows], xr_send.at[r], x_recv.at[1, r],
            device_id=(jnp.where(site == 0, 3, 0), ahead), device_id_type=MESH)

    def pass_x(count):
        def body(r, carry):
            send_xr(r).wait_recv()
            send_xon(r).start()
            return carry

        lax.fori_loop(0, count, body, 0)

    def passed_x(count):
        def body(r, carry):
            send_xon(r).wait_send()
            return carry

        lax.fori_loop(0, count, body, 0)

    def x_of(p, i):
        send_s(p, i).wait_recv()
        rows = pl.ds(pl.multiple_of(i * WIDE, WIDE), WIDE)
        x_out[p, rows] = (three[rows] + s_in[p, rows].astype(F32)).astype(BF16)
        for k in range(WIDE // ROWS):
            r = i * (WIDE // ROWS) + k
            if p == 1:
                by_site = jnp.logical_and(last, r < X_LAST)

                @pl.when(by_site)
                def _():
                    send_xr(r).start()

                @pl.when(jnp.logical_not(by_site))
                def _():
                    send_x(p, r).start()
            else:
                send_x(p, r).start()

    def cover(p):
        @pl.when(first)
        def _():
            env_load(p).wait()

            def mask(r, carry):
                rows = pl.ds(pl.multiple_of(r * ROWS, ROWS), ROWS)
                inside = jnp.logical_and(row + r * ROWS < dim_first, lane < dim_first)
                env_v[p, rows] = jnp.where(inside, env_v[p, rows].astype(F32), 0.0).astype(BF16)
                return carry

            lax.fori_loop(0, chunks, mask, 0)

    def arrive(p, i):
        for k in range(WIDE // ROWS):
            send_y(p, i * (WIDE // ROWS) + k).wait_recv()

    def move(p, s, i):
        rows = pl.ds(pl.multiple_of(i * WIDE, WIDE), WIDE)
        moved[s, rows] = (dot(env_v[p, rows], ket_v[p, s]) * on[s]).astype(BF16)

    def early(p, i):
        arrive(p, i)
        for s in range(4):
            move(p, s, i)

    def part(s, rows):
        return lax.dot_general(bra_v[s, :, rows], moved[s], (((0,), (0,)), ((), ())),
                               preferred_element_type=F32)

    def by_half(body):
        def step(h, carry):
            body(h, pl.ds(pl.multiple_of(h * HALF, HALF), HALF))
            return carry

        lax.fori_loop(0, size // HALF, step, 0)

    def single(p):
        def body(h, rows):
            s_out[p, rows] = (part(1, rows) + part(2, rows)).astype(BF16)
            for k in range(HALF // WIDE):
                send_s(p, h * (HALF // WIDE) + k).start()

        by_half(body)

    def double(p):
        def body(h, rows):
            both = part(3, rows)
            x_out[p, rows] = both.astype(BF16)
            three[rows] = both

            @pl.when(core == 1)
            def _():
                for k in range(HALF // ROWS):
                    send_x(p, h * (HALF // ROWS) + k).start()

            @pl.when(core == 0)
            def _():
                for k in range(HALF // WIDE):
                    x_of(p, h * (HALF // WIDE) + k)

        by_half(body)

    def none(p):
        def body(h, rows):
            stay[p, rows] = part(0, rows)

        by_half(body)

    def compute_first(p, i):
        rows = pl.ds(pl.multiple_of(i * WIDE, WIDE), WIDE)
        here = env_v[p]

        @pl.when(i == 0)
        def _():
            for s in (3, 1, 2, 0):
                if p == 0:
                    bra_load(s).wait()
                ket_load(p, s).wait()

        def whole(s):
            left = lax.dot_general(bra_v[s, :, rows], here, (((0,), (0,)), ((), ())),
                                   preferred_element_type=F32)
            return dot((left * on[s]).astype(BF16), ket_v[p, s])

        both = whole(3)
        x_out[p, rows] = both.astype(BF16)
        three[rows] = both
        s_out[p, rows] = (whole(1) + whole(2)).astype(BF16)
        stay[p, rows] = whole(0)
        send_s(p, i).start()
        if p == 0:
            @pl.when(core == 1)
            def _():
                for k in range(WIDE // ROWS):
                    send_x(p, i * (WIDE // ROWS) + k).start()
        else:
            @pl.when(jnp.logical_and(core == 1, i < X_FIRST // (WIDE // ROWS)))
            def _():
                for k in range(WIDE // ROWS):
                    send_xr(i * (WIDE // ROWS) + k).start()

        @pl.when(jnp.logical_and(core == 0, i > 0))
        def _():
            x_of(p, i - 1)

        @pl.when(jnp.logical_and(core == 0, i == wides - 1))
        def _():
            x_of(p, i)

    def compute_later(p, k):
        @pl.when(k == 0)
        def _():
            arrive(p, wides - 1)
            for s in (1, 2, 3, 0):
                move(p, s, wides - 1)

        @pl.when(jnp.where(core == 1, k == 2, k == 1))
        def _():
            single(p)

        @pl.when(jnp.where(core == 1, k == 1, k == 2))
        def _():
            double(p)

        @pl.when(k == 3)
        def _():
            none(p)

    def compute(p, k):
        @pl.when(first)
        def _():
            compute_first(p, k)

        @pl.when(jnp.logical_not(first))
        def _():
            compute_later(p, k)

    def finish(p, r):
        rows = pl.ds(pl.multiple_of(r * ROWS, ROWS), ROWS)

        told = jnp.logical_and(core == 1, lax.rem(r, WIDE // ROWS) == 0)
        if p == 1:
            told = jnp.logical_and(told, jnp.logical_not(jnp.logical_and(first, r == 0)))

        @pl.when(told)
        def _():
            send_s(p, r // (WIDE // ROWS)).wait_recv()

        send_x(p, r).wait_recv()
        total = stay[p, rows] + jnp.where(core == 1, s_in[p, rows].astype(F32), 0.0)
        total += jnp.where(has_before > 0, x_in[p, rows].astype(F32), 0.0)
        inside = jnp.logical_and(row + r * ROWS < dim_next, lane < dim_next)
        out[0, p, 0, rows] = jnp.where(inside, total, 0.0).astype(BF16)

        around = detour(p, r)

        @pl.when(around)
        def _():
            send_relay(p, r).start()

        @pl.when(jnp.logical_not(jnp.logical_or(last, around)))
        def _():
            send_y(p, r).start()

    turn = jnp.where(first, jnp.where(core == 1, TURN_ONE, TURN_ZERO), TURN)

    def work(t, carry):
        k = t - turn

        @pl.when(jnp.logical_and(k >= 0, k < 4))
        def _():
            @pl.when(k == 0)
            def _():
                cover(1)

            compute(1, k)

        @pl.when(t < chunks)
        def _():
            finish(0, t)

        i = t - LATE

        @pl.when(jnp.logical_and(jnp.logical_not(first), jnp.logical_and(i >= 0, i < wides - 1)))
        def _():
            @pl.when(i == 0)
            def _():
                for s in range(4):
                    ket_load(1, s).wait()

            early(1, i)

        return carry

    def first_early(i, carry):
        early(0, i)
        return carry

    def first_compute(k, carry):
        compute(0, k)
        return carry

    def last_finish(r, carry):
        finish(1, jnp.where(jnp.logical_and(last, core == 0), lax.rem(r + X_LAST, chunks), r))
        return carry

    cover(0)
    pl.semaphore_wait(barrier, 6)

    @pl.when(jnp.logical_and(site == 3, core == 0))
    def _():
        pass_on(0)
        pass_on(1)

    @pl.when(jnp.logical_and(site == 3, core == 1))
    def _():
        pass_x(X_FIRST)

    @pl.when(jnp.logical_not(first))
    def _():
        for s in range(4):
            ket_load(0, s).wait()
            bra_load(s).wait()
        lax.fori_loop(0, wides - 1, first_early, 0)

    lax.fori_loop(0, 4, first_compute, 0)

    @pl.when(first)
    def _():
        env_load(1).start()

    for s in (3, 1, 2, 0):
        ket_load(1, s).start()

    lax.fori_loop(0, jnp.maximum(turn + 4, chunks), work, 0)

    @pl.when(jnp.logical_and(first, core == 1))
    def _():
        send_s(1, 0).wait_recv()

        def send(r, carry):
            send_x(1, r).start()
            return carry

        lax.fori_loop(X_FIRST, chunks, send, 0)

    lax.fori_loop(0, chunks, last_finish, 0)

    @pl.when(jnp.logical_and(site == 1, core == 1))
    def _():
        pass_on(1)
        passed_on(1)

    @pl.when(jnp.logical_and(site == 3, core == 1))
    def _():
        passed_x(X_FIRST)

    @pl.when(jnp.logical_and(site == 0, core == 0))
    def _():
        pass_x(X_LAST)
        passed_x(X_LAST)

    @pl.when(jnp.logical_and(site == 3, core == 0))
    def _():
        passed_on(0)
        passed_on(1)

    def drain(t, carry):
        p, r = t // chunks, lax.rem(t, chunks)
        send_x(p, r).wait_send()

        @pl.when(jnp.logical_not(last))
        def _():
            send_y(p, r).wait_send()

        return carry

    lax.fori_loop(0, pairs * chunks, drain, 0)

    def drain_s(t, carry):
        send_s(t // wides, lax.rem(t, wides)).wait_send()
        return carry

    lax.fori_loop(0, pairs * wides, drain_s, 0)


def per_device(env_in, bra, ket, sector_dims, flags):
    pairs, size = env_in.shape[0], env_in.shape[-1]
    wides, chunks = size // WIDE, size // ROWS
    blocks = (pairs, size, size)
    dma = pltpu.SemaphoreType.DMA
    smem = pl.BlockSpec(memory_space=pltpu.SMEM)
    hbm = pl.BlockSpec(memory_space=pl.ANY)
    return pl.pallas_call(
        chain_kernel,
        out_shape=pltpu.VMEM((1, pairs, 1, size, size), BF16),
        in_specs=[smem, smem, hbm, hbm, hbm],
        out_specs=pl.BlockSpec(memory_space=pltpu.VMEM),
        scratch_shapes=[
            pltpu.VMEM(blocks, BF16),
            pltpu.VMEM((4, size, size), BF16),
            pltpu.VMEM((pairs, 4, size, size), BF16),
            pltpu.VMEM((4, size, size), BF16),
            pltpu.VMEM(blocks, F32),
            pltpu.VMEM((size, size), F32),
            pltpu.VMEM(blocks, BF16),
            pltpu.VMEM(blocks, BF16),
            pltpu.VMEM(blocks, BF16),
            pltpu.VMEM(blocks, BF16),
            dma((pairs,)),
            dma((4,)),
            dma((pairs, 4)),
            dma((pairs, wides)),
            dma((pairs, wides)),
            dma((pairs, chunks)),
            dma((pairs, chunks)),
            dma((pairs, chunks)),
            dma((pairs, chunks)),
            pltpu.VMEM((pairs, RELAYED * ROWS, size), BF16),
            dma((pairs, RELAYED)),
            dma((pairs, RELAYED)),
            pltpu.VMEM((max(X_FIRST, X_LAST) * ROWS, size), BF16),
            dma((max(X_FIRST, X_LAST),)),
            dma((max(X_FIRST, X_LAST),)),
        ],
        compiler_params=pltpu.CompilerParams(
            collective_id=0, has_side_effects=True, vmem_limit_bytes=56 << 20
        ),
        cost_estimate=pl.CostEstimate(
            flops=pairs * 16 * size**3, bytes_accessed=16 * size * size * 2, transcendentals=0
        ),
    )(sector_dims, jnp.swapaxes(flags, 1, 2), env_in, bra, ket)


def solution(mesh):
    in_specs = (
        P(None, "sector", None, None),
        P("site", None, "sector", None, None),
        P("site", None, None, "sector", None, None),
        P(),
        P("site", None, "sector"),
    )
    out_specs = P("site", None, "sector", None, None)
    return jax.shard_map(
        per_device, mesh=mesh, in_specs=in_specs, out_specs=out_specs, check_vma=False
    )
```

```python
import jax
import jax.numpy as jnp
from jax import lax
from jax.experimental import pallas as pl
from jax.experimental.pallas import tpu as pltpu
from jax.sharding import PartitionSpec as P

MESH = pl.DeviceIdType.MESH
WIDE = 128
HALF = 256
ROWS = 64
TURN = 8
TURN_ZERO = 4
TURN_ONE = 4
X_FIRST = 6
X_LAST = 2
RELAYED = 3
LATE = 5
F32 = jnp.float32
BF16 = jnp.bfloat16


def chain_kernel(
    dims, flags, env, bra, ket, out,
    env_v, bra_v, ket_v, moved, stay, three, s_out, s_in, x_out, x_in,
    env_sem, bra_sem, ket_sem, s_send, s_recv, x_send, x_recv, y_send, y_recv,
    relay, relay_send, relay_recv, x_relay, xr_send, xr_recv,
):
    site, sector = lax.axis_index("site"), lax.axis_index("sector")
    sites, sectors = lax.axis_size("site"), lax.axis_size("sector")
    core = lax.rem(sector, 2)
    pairs, size = env_v.shape[0], env_v.shape[1]
    wides, chunks = size // WIDE, size // ROWS
    other = sector + 1 - 2 * core
    ahead = lax.rem(sector + 2, sectors)
    behind = lax.rem(sector + sectors - 2, sectors)
    first, last = site == 0, site == sites - 1

    def env_load(p):
        return pltpu.make_async_copy(env.at[p, 0], env_v.at[p], env_sem.at[p])

    def bra_load(s):
        return pltpu.make_async_copy(bra.at[0, s, 0], bra_v.at[s], bra_sem.at[s])

    def ket_load(p, s):
        return pltpu.make_async_copy(ket.at[0, p, s, 0], ket_v.at[p, s], ket_sem.at[p, s])

    def send_s(p, i):
        rows = pl.ds(pl.multiple_of(i * WIDE, WIDE), WIDE)
        return pltpu.make_async_remote_copy(
            s_out.at[p, rows], s_in.at[p, rows], s_send.at[p, i], s_recv.at[p, i],
            device_id=(site, other), device_id_type=MESH)

    def send_x(p, r):
        rows = pl.ds(pl.multiple_of(r * ROWS, ROWS), ROWS)
        return pltpu.make_async_remote_copy(
            x_out.at[p, rows], x_in.at[p, rows], x_send.at[p, r], x_recv.at[p, r],
            device_id=(site, ahead), device_id_type=MESH)

    def detour(p, r):
        return jnp.logical_and(jnp.logical_and(core == 1, r < RELAYED), site == 1)

    def send_y(p, r):
        rows = pl.ds(pl.multiple_of(r * ROWS, ROWS), ROWS)
        return pltpu.make_async_remote_copy(
            out.at[0, p, 0, rows], env_v.at[p, rows], y_send.at[p, r], y_recv.at[p, r],
            device_id=(lax.rem(site + 1, sites), sector), device_id_type=MESH)

    def send_relay(p, r):
        rows = pl.ds(pl.multiple_of(r * ROWS, ROWS), ROWS)
        return pltpu.make_async_remote_copy(
            out.at[0, p, 0, rows], relay.at[p, rows], y_send.at[p, r], relay_recv.at[p, r],
            device_id=(3, other), device_id_type=MESH)

    def send_on(p, r):
        rows = pl.ds(pl.multiple_of(r * ROWS, ROWS), ROWS)
        return pltpu.make_async_remote_copy(
            relay.at[p, rows], env_v.at[p, rows], relay_send.at[p, r], y_recv.at[p, r],
            device_id=(2, other), device_id_type=MESH)

    def pass_on(p):
        def body(r, carry):
            send_relay(p, r).wait_recv()
            send_on(p, r).start()
            return carry

        lax.fori_loop(0, RELAYED, body, 0)

    def passed_on(p):
        def body(r, carry):
            send_on(p, r).wait_send()
            return carry

        lax.fori_loop(0, RELAYED, body, 0)

    barrier = pltpu.get_barrier_semaphore()
    for partner in (other, ahead, behind):
        pl.semaphore_signal(barrier, inc=1, device_id=(site, partner), device_id_type=MESH)
    for partner in (lax.rem(site + 1, sites), lax.rem(site + sites - 1, sites)):
        pl.semaphore_signal(barrier, inc=1, device_id=(partner, sector), device_id_type=MESH)
    pl.semaphore_signal(barrier, inc=1, device_id=(lax.rem(site + 2, sites), other), device_id_type=MESH)

    @pl.when(first)
    def _():
        env_load(0).start()

    for s in (3, 1, 2, 0):
        bra_load(s).start()
        ket_load(0, s).start()

    dim_first, dim_next = dims[0, sector], dims[site + 1, sector]
    on = [flags[0, 0, s].astype(F32) for s in range(4)]
    has_before = (sector >= 2).astype(jnp.int32)
    lane = lax.broadcasted_iota(jnp.int32, (ROWS, size), 1)
    row = lax.broadcasted_iota(jnp.int32, (ROWS, size), 0)

    def dot(a, b):
        return jnp.dot(a, b, preferred_element_type=F32)

    def send_xr(r):
        rows = pl.ds(pl.multiple_of(r * ROWS, ROWS), ROWS)
        return pltpu.make_async_remote_copy(
            x_out.at[1, rows], x_relay.at[rows], x_send.at[1, r], xr_recv.at[r],
            device_id=(jnp.where(site == 0, 3, 0), sector), device_id_type=MESH)

    def send_xon(r):
        rows = pl.ds(pl.multiple_of(r * ROWS, ROWS), ROWS)
        return pltpu.make_async_remote_copy(
            x_relay.at[rows], x_in.at[1, rows], xr_send.at[r], x_recv.at[1, r],
            device_id=(jnp.where(site == 0, 3, 0), ahead), device_id_type=MESH)

    def pass_x(count):
        def body(r, carry):
            send_xr(r).wait_recv()
            send_xon(r).start()
            return carry

        lax.fori_loop(0, count, body, 0)

    def passed_x(count):
        def body(r, carry):
            send_xon(r).wait_send()
            return carry

        lax.fori_loop(0, count, body, 0)

    def x_of(p, i):
        send_s(p, i).wait_recv()
        rows = pl.ds(pl.multiple_of(i * WIDE, WIDE), WIDE)
        x_out[p, rows] = (three[rows] + s_in[p, rows].astype(F32)).astype(BF16)
        for k in range(WIDE // ROWS):
            r = i * (WIDE // ROWS) + k
            if p == 1:
                by_site = jnp.logical_and(last, r < X_LAST)

                @pl.when(by_site)
                def _():
                    send_xr(r).start()

                @pl.when(jnp.logical_not(by_site))
                def _():
                    send_x(p, r).start()
            else:
                send_x(p, r).start()

    def cover(p):
        @pl.when(first)
        def _():
            env_load(p).wait()

            def mask(r, carry):
                rows = pl.ds(pl.multiple_of(r * ROWS, ROWS), ROWS)
                inside = jnp.logical_and(row + r * ROWS < dim_first, lane < dim_first)
                env_v[p, rows] = jnp.where(inside, env_v[p, rows].astype(F32), 0.0).astype(BF16)
                return carry

            lax.fori_loop(0, chunks, mask, 0)

    def arrive(p, i):
        for k in range(WIDE // ROWS):
            send_y(p, i * (WIDE // ROWS) + k).wait_recv()

    def move(p, s, i):
        rows = pl.ds(pl.multiple_of(i * WIDE, WIDE), WIDE)
        moved[s, rows] = (dot(env_v[p, rows], ket_v[p, s]) * on[s]).astype(BF16)

    def early(p, i):
        arrive(p, i)
        for s in range(4):
            move(p, s, i)

    def part(s, rows):
        return lax.dot_general(bra_v[s, :, rows], moved[s], (((0,), (0,)), ((), ())),
                               preferred_element_type=F32)

    def by_half(body):
        def step(h, carry):
            body(h, pl.ds(pl.multiple_of(h * HALF, HALF), HALF))
            return carry

        lax.fori_loop(0, size // HALF, step, 0)

    def single(p):
        def body(h, rows):
            s_out[p, rows] = (part(1, rows) + part(2, rows)).astype(BF16)
            for k in range(HALF // WIDE):
                send_s(p, h * (HALF // WIDE) + k).start()

        by_half(body)

    def double(p):
        def body(h, rows):
            both = part(3, rows)
            x_out[p, rows] = both.astype(BF16)
            three[rows] = both

            @pl.when(core == 1)
            def _():
                for k in range(HALF // ROWS):
                    send_x(p, h * (HALF // ROWS) + k).start()

            @pl.when(core == 0)
            def _():
                for k in range(HALF // WIDE):
                    x_of(p, h * (HALF // WIDE) + k)

        by_half(body)

    def none(p):
        def body(h, rows):
            stay[p, rows] = part(0, rows)

        by_half(body)

    def compute_first(p, i):
        rows = pl.ds(pl.multiple_of(i * WIDE, WIDE), WIDE)
        here = env_v[p]

        @pl.when(i == 0)
        def _():
            for s in (3, 1, 2, 0):
                if p == 0:
                    bra_load(s).wait()
                ket_load(p, s).wait()

        def whole(s):
            left = lax.dot_general(bra_v[s, :, rows], here, (((0,), (0,)), ((), ())),
                                   preferred_element_type=F32)
            return dot((left * on[s]).astype(BF16), ket_v[p, s])

        both = whole(3)
        x_out[p, rows] = both.astype(BF16)
        three[rows] = both
        s_out[p, rows] = (whole(1) + whole(2)).astype(BF16)
        stay[p, rows] = whole(0)
        send_s(p, i).start()
        if p == 0:
            @pl.when(core == 1)
            def _():
                for k in range(WIDE // ROWS):
                    send_x(p, i * (WIDE // ROWS) + k).start()
        else:
            @pl.when(jnp.logical_and(core == 1, i < X_FIRST // (WIDE // ROWS)))
            def _():
                for k in range(WIDE // ROWS):
                    send_xr(i * (WIDE // ROWS) + k).start()

        @pl.when(jnp.logical_and(core == 0, i > 0))
        def _():
            x_of(p, i - 1)

        @pl.when(jnp.logical_and(core == 0, i == wides - 1))
        def _():
            x_of(p, i)

    def compute_later(p, k):
        @pl.when(k == 0)
        def _():
            arrive(p, wides - 1)
            for s in (1, 2, 3, 0):
                move(p, s, wides - 1)

        @pl.when(jnp.where(core == 1, k == 2, k == 1))
        def _():
            single(p)

        @pl.when(jnp.where(core == 1, k == 1, k == 2))
        def _():
            double(p)

        @pl.when(k == 3)
        def _():
            none(p)

    def compute(p, k):
        @pl.when(first)
        def _():
            compute_first(p, k)

        @pl.when(jnp.logical_not(first))
        def _():
            compute_later(p, k)

    def finish(p, r):
        rows = pl.ds(pl.multiple_of(r * ROWS, ROWS), ROWS)

        told = jnp.logical_and(core == 1, lax.rem(r, WIDE // ROWS) == 0)
        if p == 1:
            told = jnp.logical_and(told, jnp.logical_not(jnp.logical_and(first, r == 0)))

        @pl.when(told)
        def _():
            send_s(p, r // (WIDE // ROWS)).wait_recv()

        send_x(p, r).wait_recv()
        total = stay[p, rows] + jnp.where(core == 1, s_in[p, rows].astype(F32), 0.0)
        total += jnp.where(has_before > 0, x_in[p, rows].astype(F32), 0.0)
        inside = jnp.logical_and(row + r * ROWS < dim_next, lane < dim_next)
        out[0, p, 0, rows] = jnp.where(inside, total, 0.0).astype(BF16)

        around = detour(p, r)

        @pl.when(around)
        def _():
            send_relay(p, r).start()

        @pl.when(jnp.logical_not(jnp.logical_or(last, around)))
        def _():
            send_y(p, r).start()

    turn = jnp.where(first, jnp.where(core == 1, TURN_ONE, TURN_ZERO), TURN)

    def work(t, carry):
        k = t - turn

        @pl.when(jnp.logical_and(k >= 0, k < 4))
        def _():
            @pl.when(k == 0)
            def _():
                cover(1)

            compute(1, k)

        @pl.when(t < chunks)
        def _():
            finish(0, t)

        i = t - LATE

        @pl.when(jnp.logical_and(jnp.logical_not(first), jnp.logical_and(i >= 0, i < wides - 1)))
        def _():
            @pl.when(i == 0)
            def _():
                for s in range(4):
                    ket_load(1, s).wait()

            early(1, i)

        return carry

    def first_early(i, carry):
        early(0, i)
        return carry

    def first_compute(k, carry):
        compute(0, k)
        return carry

    def last_finish(r, carry):
        finish(1, jnp.where(jnp.logical_and(last, core == 0), lax.rem(r + X_LAST, chunks), r))
        return carry

    cover(0)
    pl.semaphore_wait(barrier, 6)

    @pl.when(jnp.logical_and(site == 3, core == 0))
    def _():
        pass_on(0)
        pass_on(1)

    @pl.when(jnp.logical_and(site == 3, core == 1))
    def _():
        pass_x(X_FIRST)

    @pl.when(jnp.logical_not(first))
    def _():
        for s in range(4):
            ket_load(0, s).wait()
            bra_load(s).wait()
        lax.fori_loop(0, wides - 1, first_early, 0)

    lax.fori_loop(0, 4, first_compute, 0)

    @pl.when(first)
    def _():
        env_load(1).start()

    for s in (3, 1, 2, 0):
        ket_load(1, s).start()

    lax.fori_loop(0, jnp.maximum(turn + 4, chunks), work, 0)

    @pl.when(jnp.logical_and(first, core == 1))
    def _():
        send_s(1, 0).wait_recv()

        def send(r, carry):
            send_x(1, r).start()
            return carry

        lax.fori_loop(X_FIRST, chunks, send, 0)

    lax.fori_loop(0, chunks, last_finish, 0)

    @pl.when(jnp.logical_and(site == 3, core == 1))
    def _():
        passed_x(X_FIRST)

    @pl.when(jnp.logical_and(site == 0, core == 0))
    def _():
        pass_x(X_LAST)
        passed_x(X_LAST)

    @pl.when(jnp.logical_and(site == 3, core == 0))
    def _():
        passed_on(0)
        passed_on(1)

    def drain(t, carry):
        p, r = t // chunks, lax.rem(t, chunks)
        send_x(p, r).wait_send()

        @pl.when(jnp.logical_not(last))
        def _():
            send_y(p, r).wait_send()

        return carry

    lax.fori_loop(0, pairs * chunks, drain, 0)

    def drain_s(t, carry):
        send_s(t // wides, lax.rem(t, wides)).wait_send()
        return carry

    lax.fori_loop(0, pairs * wides, drain_s, 0)


def per_device(env_in, bra, ket, sector_dims, flags):
    pairs, size = env_in.shape[0], env_in.shape[-1]
    wides, chunks = size // WIDE, size // ROWS
    blocks = (pairs, size, size)
    dma = pltpu.SemaphoreType.DMA
    smem = pl.BlockSpec(memory_space=pltpu.SMEM)
    hbm = pl.BlockSpec(memory_space=pl.ANY)
    return pl.pallas_call(
        chain_kernel,
        out_shape=pltpu.VMEM((1, pairs, 1, size, size), BF16),
        in_specs=[smem, smem, hbm, hbm, hbm],
        out_specs=pl.BlockSpec(memory_space=pltpu.VMEM),
        scratch_shapes=[
            pltpu.VMEM(blocks, BF16),
            pltpu.VMEM((4, size, size), BF16),
            pltpu.VMEM((pairs, 4, size, size), BF16),
            pltpu.VMEM((4, size, size), BF16),
            pltpu.VMEM(blocks, F32),
            pltpu.VMEM((size, size), F32),
            pltpu.VMEM(blocks, BF16),
            pltpu.VMEM(blocks, BF16),
            pltpu.VMEM(blocks, BF16),
            pltpu.VMEM(blocks, BF16),
            dma((pairs,)),
            dma((4,)),
            dma((pairs, 4)),
            dma((pairs, wides)),
            dma((pairs, wides)),
            dma((pairs, chunks)),
            dma((pairs, chunks)),
            dma((pairs, chunks)),
            dma((pairs, chunks)),
            pltpu.VMEM((pairs, RELAYED * ROWS, size), BF16),
            dma((pairs, RELAYED)),
            dma((pairs, RELAYED)),
            pltpu.VMEM((max(X_FIRST, X_LAST) * ROWS, size), BF16),
            dma((max(X_FIRST, X_LAST),)),
            dma((max(X_FIRST, X_LAST),)),
        ],
        compiler_params=pltpu.CompilerParams(
            collective_id=0, has_side_effects=True, vmem_limit_bytes=56 << 20
        ),
        cost_estimate=pl.CostEstimate(
            flops=pairs * 16 * size**3, bytes_accessed=16 * size * size * 2, transcendentals=0
        ),
    )(sector_dims, jnp.swapaxes(flags, 1, 2), env_in, bra, ket)


def solution(mesh):
    in_specs = (
        P(None, "sector", None, None),
        P("site", None, "sector", None, None),
        P("site", None, None, "sector", None, None),
        P(),
        P("site", None, "sector"),
    )
    out_specs = P("site", None, "sector", None, None)
    return jax.shard_map(
        per_device, mesh=mesh, in_specs=in_specs, out_specs=out_specs, check_vma=False
    )
```
